128 devices in a mesh: row: 8 (over y_hi, z), col: 16 (over x, y_lo, core).
Axes of the slice: x: 4, y: 4 (y_hi: 2, y_lo: 2; y = y_hi * 2 + y_lo), z: 4, core: 2. Of those that a mesh axis runs over, the one named last changes fastest.
Arguments:
- integrals: float32 [16384, 32768], P('row', 'col'), may hold values from -0.03125 to 0.03125
- amplitudes: float32 [32768, 1024], P('col', 'row'), may hold values from -6 to 6
- source_order: int32 [1024], replicated, may hold values from 0 to 1023, each once
- target_order: int32 [1024], replicated, may hold values from 0 to 1023, each once
Outputs:
- ladder: float32 [1024, 16384], P('col', 'row')
The draws below stay inside these ranges and needn't reach their ends.
Inputs may be any that keep to these rules, and one draw needn't show every extreme that they name: `source_order`: each of 0 .. 1023 appears exactly once. `target_order`: each of 0 .. 1023 appears exactly once.
All inputs are finite; a program needn't handle non-finite values.
Results may differ from the reference program's by a relative error of at most 0.00007.
Values sent between devices are 32-bit elements; how exact they have to be, the bound alone decides.
No kernel may reach another device: no remote copies, remote signals or barrier semaphores. Data moves between devices by JAX's collectives and lax.ppermute only.
A program may use at most 128 MiB of HBM per device.

```python
import jax
import jax.numpy as jnp
from jax import lax

IJ = 1024
AB = 16384
CD = 32768


def raised(array, rng, source, target, parts, factor):
    def block_of(dim):
        return (jnp.arange(array.shape[dim]) // (array.shape[dim] // parts)).reshape((-1,) + (1,) * (array.ndim - 1 - dim))

    first = jax.random.permutation(rng, parts)[block_of(target)]
    second = (block_of(target) + parts // 2) % parts
    return jnp.where((block_of(source) == first) | (block_of(source) == second), factor * array, array)


def shard_levels(own_key, shape, shards, least, high):
    gain, own = 1.0, jax.random.fold_in(own_key, 6)
    for axis_at, parts in shards:
        heights = jnp.exp(jax.random.uniform(jax.random.fold_in(own, axis_at), (parts,), jnp.float32, least / len(shards), high / len(shards)))
        gain = gain * jnp.repeat(heights, shape[axis_at] // parts).reshape([-1 if axis == axis_at else 1 for axis in range(len(shape))])
    return gain


def scatter_about(key, shape, deviation, reach, split=(), kind=jnp.bfloat16):
    entries = deviation * jax.random.normal(key, shape, jnp.float32)
    if split:
        entries = entries * shard_levels(key, shape, split, -0.22, 0.18)
    return jnp.clip(entries, -reach, reach).astype(kind)


def heavy_noise(rng, extent, width, limit, shards, heavy, kind=jnp.bfloat16):
    result = width * jax.random.normal(rng, extent, jnp.float32)
    if shards:
        result = result * shard_levels(rng, extent, shards, -0.22, 0.18)
    return jnp.clip(raised(result, jax.random.fold_in(rng, 3), *heavy), -limit, limit).astype(kind)


def setup_inputs(seed: int = 0) -> dict:
    key_of = jax.random.split(jax.random.key(seed), 5)
    integrals = scatter_about(key_of[0], (AB, CD), CD ** -0.5, 0.03125, ((0, 8), (1, 16)), jnp.float32)
    amplitudes = heavy_noise(key_of[1], (CD, IJ), 1.0, 6.0, ((0, 16), (1, 8)), (0, 1, 16, 2.0), jnp.float32)
    source_order = jax.random.permutation(key_of[2], IJ).astype(jnp.int32)
    target_order = jax.random.permutation(key_of[3], IJ).astype(jnp.int32)
    return dict(integrals=integrals, amplitudes=amplitudes, source_order=source_order, target_order=target_order)


def reference(integrals, amplitudes, source_order, target_order):
    length = target_order.shape[0]
    inverse = jnp.zeros((length,), jnp.int32).at[source_order].set(jnp.arange(length, dtype=jnp.int32))
    columns = jnp.take(inverse, target_order)
    ordered = jnp.take(amplitudes, columns, axis=1)
    return lax.dot_general(ordered, integrals, (((0,), (1,)), ((), ())), precision=lax.Precision.HIGHEST, preferred_element_type=jnp.float32)
```

```python
import functools

import jax
import jax.numpy as jnp
from jax import lax
from jax.experimental import pallas as pl
from jax.experimental.pallas import tpu as pltpu
from jax.sharding import PartitionSpec as P

AXES = ("row", "col")
NT = (((1,), (1,)), ((), ()))
X_ROWS = 32
MIB = 1 << 20


def device_index(x, y, z, core):
    return ((y // 2) * 4 + z) * 16 + (x * 2 + y % 2) * 2 + core


def shift(array, dx=0, dy=0, dz=0, flip_y=False, flip_core=False):
    pairs = []
    for x in range(4):
        for y in range(4):
            for z in range(4):
                for core in range(2):
                    to_y = y ^ 1 if flip_y else (y + dy) % 4
                    to = device_index((x + dx) % 4, to_y, (z + dz) % 4, core ^ int(flip_core))
                    pairs.append((device_index(x, y, z, core), to))
    return lax.ppermute(array, AXES, pairs)


def place():
    row, col = lax.axis_index("row"), lax.axis_index("col")
    return col // 4, (col // 2) % 2, col % 2, row // 4, row % 4


def rolled(array, start):
    sizes = array.shape
    return lax.dynamic_slice(jnp.concatenate([array, array]), (start,) + (0,) * (array.ndim - 1), sizes)


def flipped(array, bit, axis):
    return jnp.where(bit == 0, array, jnp.flip(array, axis))


def select_kernel(n, choose_ref, *refs):
    pieces, last_a, last_b, outs = refs[:7], refs[7], refs[8], refs[9:]
    last = jnp.where(pl.program_id(0) == 0, last_a[...], last_b[...])
    block = jnp.concatenate([p[...] for p in pieces] + [last], axis=1)
    high = block.astype(jnp.bfloat16)
    low = (block - high.astype(jnp.float32)).astype(jnp.bfloat16)
    for part, (x_ref, y_ref) in ((high, outs[:2]), (low, outs[2:])):
        rows = lax.dot_general(choose_ref[...], part, NT, preferred_element_type=jnp.float32)
        rows = rows.astype(jnp.bfloat16)
        x_ref[...] = rows[:n]
        y_ref[...] = rows[n:]


def select(choose, pieces, last_a, last_b, n):
    k = pieces[0].shape[0]
    half = k // 2
    q = choose.shape[0]
    piece = pl.BlockSpec((half, 128), lambda i: (i, 0))
    whole = pl.BlockSpec((half, 128), lambda i: (0, 0))
    shapes = [(n, k), (q - n, k)] * 2
    return pl.pallas_call(
        functools.partial(select_kernel, n),
        grid=(2,),
        in_specs=[pl.BlockSpec(choose.shape, lambda i: (0, 0))] + [piece] * 7 + [whole] * 2,
        out_specs=[pl.BlockSpec((s[0], half), lambda i: (0, i)) for s in shapes],
        out_shape=[jax.ShapeDtypeStruct(s, jnp.bfloat16) for s in shapes],
        compiler_params=pltpu.CompilerParams(vmem_limit_bytes=48 * MIB),
        cost_estimate=pl.CostEstimate(flops=4 * q * 1024 * k, bytes_accessed=8 * q * k, transcendentals=0),
        name="select",
    )(choose, *pieces, last_a, last_b)


def contract_kernel(v_ref, ha_ref, la_ref, hb_ref, lb_ref, keep_ref, send_ref):
    v = v_ref[...]
    high = v.astype(jnp.bfloat16)
    low = (v - high.astype(jnp.float32)).astype(jnp.bfloat16)
    k = ha_ref.shape[1]
    dot = functools.partial(lax.dot_general, dimension_numbers=NT, preferred_element_type=jnp.float32)
    total = None
    for h_ref, l_ref, at in ((ha_ref, la_ref, 0), (hb_ref, lb_ref, k)):
        hv, lv = high[:, at : at + k], low[:, at : at + k]
        term = dot(h_ref[...], hv) + dot(h_ref[...], lv) + dot(l_ref[...], hv)
        total = term if total is None else total + term
    half = keep_ref.shape[0]
    keep_ref[...] = total[:half]
    send_ref[...] = total[half:]


def contract(v, ha, la, hb, lb, tile=256):
    n, k = ha.shape
    ab, cd = v.shape
    whole = pl.BlockSpec((n, k), lambda i: (0, 0))
    return pl.pallas_call(
        contract_kernel,
        grid=(ab // tile,),
        in_specs=[pl.BlockSpec((tile, cd), lambda i: (i, 0))] + [whole] * 4,
        out_specs=[pl.BlockSpec((n // 2, tile), lambda i: (0, i))] * 2,
        out_shape=[jax.ShapeDtypeStruct((n // 2, ab), jnp.float32)] * 2,
        compiler_params=pltpu.CompilerParams(vmem_limit_bytes=48 * MIB),
        cost_estimate=pl.CostEstimate(
            flops=6 * n * ab * cd, bytes_accessed=4 * (ab * cd + n * ab + n * cd), transcendentals=0
        ),
        name="contract",
    )(v, ha, la, hb, lb)


def gather(a):
    half = a.shape[0] // 2
    first, second = a[:half], a[half:]
    y_first = shift(first, dy=2)
    second_m = shift(second, dz=1)
    second_p = shift(second, dz=-1)
    first_m = shift(first, dz=1)
    first_p = shift(first, dz=-1)
    y_second = shift(second, dy=2)
    second_2 = shift(second_p, dz=-1)
    first_2 = shift(first_m, dz=1)
    y_second_m = shift(second_m, dy=2)
    y_second_p = shift(second_p, dy=2)
    y_first_m = shift(y_first, dz=1)
    y_first_p = shift(y_first, dz=-1)
    y_first_2a = shift(y_first_m[: half // 2], dz=1)
    y_first_2b = shift(y_first_p[half // 2 :], dz=-1)
    y_second_2 = shift(second_2, dy=2)
    firsts = [first, first_p, first_2, first_m, y_first, y_first_p, y_first_m]
    seconds = [second, second_p, second_2, second_m, y_second, y_second_p, y_second_m]
    return (firsts, y_first_2a, y_first_2b), (seconds, y_second_2[: half // 2], y_second_2[half // 2 :])


def sum_x(blocks):
    half = blocks[2].shape[0] // 2
    up, down = shift(blocks[2][:half], dx=1), shift(blocks[2][half:], dx=-1)
    one = jnp.concatenate([blocks[1][:half] + up, blocks[1][half:]])
    three = jnp.concatenate([blocks[3][:half], blocks[3][half:] + down])
    return blocks[0] + shift(one, dx=1) + shift(three, dx=-1)


def local(integrals, amplitudes, source_order, target_order):
    x, y_lo, core, y_hi, z = place()
    wanted = flipped(flipped(rolled(target_order.reshape(4, 2, 2, 64), x), y_lo, 1), core, 2)
    wanted_x = wanted[..., :X_ROWS].transpose(2, 0, 1, 3).reshape(-1)
    wanted_y = wanted[..., X_ROWS:].transpose(2, 1, 0, 3).reshape(-1)
    wanted = jnp.concatenate([wanted_x, wanted_y])
    held = flipped(rolled(source_order.reshape(2, 4, 128).transpose(1, 0, 2), z), y_hi, 1)
    held = held.transpose(1, 0, 2)
    order = jnp.concatenate([held[0].reshape(-1), held[1, 0], held[1, 1], held[1, 3], held[1, 2]])
    choose = (wanted[:, None] == order[None, :]).astype(jnp.bfloat16)

    first, second = gather(amplitudes)
    n = 16 * X_ROWS
    hxa, hya, lxa, lya = select(choose, *first, n)
    hxb, hyb, lxb, lyb = select(choose, *second, n)

    keep_y, send_y = contract(integrals, hya, lya, hyb, lyb)
    got_y = shift(send_y, flip_core=True)
    keep_x, send_x = contract(integrals, hxa, lxa, hxb, lxb)
    got_x = shift(send_x, flip_core=True)

    half = keep_y.shape[0] // 2
    y_one = keep_y[half:] + got_y[half:]
    y_own = keep_y[:half] + got_y[:half]
    y_sum = y_own + shift(y_one, flip_y=True)
    part = half // 4
    out_y = sum_x([y_sum[part * d : part * (d + 1)] for d in range(4)])

    part = keep_x.shape[0] // 4
    x_sum = sum_x([keep_x[part * d : part * (d + 1)] + got_x[part * d : part * (d + 1)] for d in range(4)])
    out_x = x_sum[: part // 2] + shift(x_sum[part // 2 :], flip_y=True)
    return jnp.concatenate([out_x, out_y])


def solution(mesh):
    in_specs = (P("row", "col"), P("col", "row"), P(), P())
    return jax.shard_map(local, mesh=mesh, in_specs=in_specs, out_specs=P("col", "row"), check_vma=False)
```

```python
import functools

import jax
import jax.numpy as jnp
from jax import lax
from jax.experimental import pallas as pl
from jax.experimental.pallas import tpu as pltpu
from jax.sharding import PartitionSpec as P

AXES = ("row", "col")
NT = (((1,), (1,)), ((), ()))
X_ROWS = 40
MIB = 1 << 20
WHOLE = pl.BlockSpec(memory_space=pltpu.VMEM)


def device_index(x, y, z, core):
    return ((y // 2) * 4 + z) * 16 + (x * 2 + y % 2) * 2 + core


def shift(array, dx=0, dy=0, dz=0, flip_y=False, flip_core=False):
    pairs = []
    for x in range(4):
        for y in range(4):
            for z in range(4):
                for core in range(2):
                    to_y = y ^ 1 if flip_y else (y + dy) % 4
                    to = device_index((x + dx) % 4, to_y, (z + dz) % 4, core ^ int(flip_core))
                    pairs.append((device_index(x, y, z, core), to))
    return lax.ppermute(array, AXES, pairs)


def place():
    row, col = lax.axis_index("row"), lax.axis_index("col")
    return col // 4, (col // 2) % 2, col % 2, row // 4, row % 4


def rolled(array, start):
    sizes = array.shape
    return lax.dynamic_slice(jnp.concatenate([array, array]), (start,) + (0,) * (array.ndim - 1), sizes)


def flipped(array, bit, axis):
    return jnp.where(bit == 0, array, jnp.flip(array, axis))


def parts_of(array):
    high = array.astype(jnp.bfloat16)
    return high, (array - high.astype(jnp.float32)).astype(jnp.bfloat16)


def stack_columns(layout, blocks, both):
    width = both.shape[1] // 2
    for at, start, size, row, col in layout:
        high, low = parts_of(blocks[at][start : start + size, :])
        both[row : row + size, col : col + 128] = high
        both[row : row + size, width + col : width + col + 128] = low


def product(vh, vl, both):
    width = both.shape[1] // 2
    dot = functools.partial(jnp.dot, preferred_element_type=jnp.float32)
    if width == 128:
        pair = dot(vh, both[...])
        return pair[:, :width] + pair[:, width:] + dot(vl, both[:, :width])
    return dot(vh, both[:, :width]) + dot(vh, both[:, width:]) + dot(vl, both[:, :width])


def first_kernel(layout, tile, v_ref, a_ref, out_h, out_l, vh_ref, vl_ref, both):
    stack_columns(layout, [a_ref], both)

    @pl.loop(0, v_ref.shape[0] // tile)
    def _(i):
        rows = pl.ds(pl.multiple_of(i * tile, tile), tile)
        vh, vl = parts_of(v_ref[rows, :])
        vh_ref[rows, :], vl_ref[rows, :] = vh, vl
        out_h[rows, :], out_l[rows, :] = parts_of(product(vh, vl, both))


def contract_kernel(layout, n, tile, vh_ref, vl_ref, *refs):
    blocks, (out_h, out_l, _, _, both) = refs[:n], refs[n:]
    stack_columns(layout, blocks, both)

    @pl.loop(0, out_h.shape[0] // tile)
    def _(i):
        rows = pl.ds(pl.multiple_of(i * tile, tile), tile)
        out_h[rows, :], out_l[rows, :] = parts_of(product(vh_ref[rows, :], vl_ref[rows, :], both))


def contract(v, columns, tile=1024):
    arrays, layout = [], []
    for i, stack in enumerate(columns):
        row = 0
        for array, start, size in stack:
            at = next((j for j, other in enumerate(arrays) if other is array), len(arrays))
            if at == len(arrays):
                arrays.append(array)
            layout.append((at, start, size, row, 128 * i))
            row += size
    ab, cd = v[0].shape
    width = 128 * len(columns)
    if len(v) == 1:
        kernel = functools.partial(first_kernel, layout, tile // 2)
    else:
        kernel = functools.partial(contract_kernel, layout, len(arrays), tile)
    inputs = [pltpu.with_memory_space_constraint(x, pltpu.VMEM) for x in (*v, *arrays)]
    out_h, out_l, *v = pl.pallas_call(
        kernel,
        in_specs=[WHOLE] * len(inputs),
        out_specs=[WHOLE] * 4,
        out_shape=[pltpu.VMEM((ab, width), jnp.bfloat16)] * 2 + [pltpu.VMEM((ab, cd), jnp.bfloat16)] * 2,
        input_output_aliases={} if len(v) == 1 else {0: 2, 1: 3},
        scratch_shapes=[pltpu.VMEM((cd, 2 * width), jnp.bfloat16)],
        compiler_params=pltpu.CompilerParams(vmem_limit_bytes=16 * MIB),
        cost_estimate=pl.CostEstimate(flops=6 * width * ab * cd, bytes_accessed=0, transcendentals=0),
        name="contract",
    )(*inputs)
    return [out_h, out_l], v


def order_kernel(n_products, n_got, tile, choose_ref, *refs):
    products, refs = refs[:n_products], refs[n_products:]
    got, outs = refs[:n_got], refs[n_got:]

    @pl.loop(0, products[0].shape[0] // tile)
    def _(i):
        some = pl.ds(pl.multiple_of(i * tile, tile), tile)
        total, at = None, 0
        for high, low in zip(products[::2], products[1::2], strict=True):
            chosen = choose_ref[:, at : at + high.shape[1]]
            at += high.shape[1]
            for part in (high, low):
                term = lax.dot_general(chosen, part[some, :], NT, preferred_element_type=jnp.float32)
                total = term if total is None else total + term
        for ref in got:
            total = total + ref[:, some]
        row = 0
        for ref in outs:
            ref[:, some] = total[row : row + ref.shape[0]]
            row += ref.shape[0]


def order(choose, products, got=(), n_outs=1, tile=1024):
    n, p = choose.shape
    ab = products[0].shape[0]
    inputs = [pltpu.with_memory_space_constraint(a, pltpu.VMEM) for a in (choose, *products, *got)]
    return pl.pallas_call(
        functools.partial(order_kernel, len(products), len(got), tile),
        in_specs=[WHOLE] * len(inputs),
        out_specs=[WHOLE] * n_outs,
        out_shape=[pltpu.VMEM((n // n_outs, ab), jnp.float32)] * n_outs,
        compiler_params=pltpu.CompilerParams(vmem_limit_bytes=16 * MIB),
        cost_estimate=pl.CostEstimate(flops=4 * n * ab * p, bytes_accessed=0, transcendentals=0),
        name="order",
    )(*inputs)


def gather(a):
    n, mid = a.shape[0], a.shape[0] // 2
    zp, zm = shift(a, dz=-1), shift(a, dz=1)
    y0 = shift(a, dy=2)
    y_rest = shift(jnp.concatenate([zm[mid:], zp[mid:]]), dy=2)
    up = shift(jnp.concatenate([zm[:mid], y0[:mid]]), dz=1)
    down = shift(jnp.concatenate([zp[mid:], y0[:mid]]), dz=-1)
    y_z2a, y_z2b = shift(up[mid:], dz=1), shift(y_rest[mid:], dz=-1)
    return (
        ([(a, 0, n)],),
        ([(zm, 0, n)], [(zp, 0, n)]),
        ([(y0, 0, n)],),
        ([(up, 0, mid), (down, 0, mid)], [(up, mid, mid), (y_rest, 0, mid)]),
        ([(down, mid, mid), (y_rest, mid, mid)], [(y_z2a, 0, mid), (y_z2b, 0, mid)]),
    )


def sum_x(blocks):
    return blocks[0] + shift(blocks[2], dx=2) + shift(blocks[1], dx=1) + shift(blocks[3], dx=-1)


def local(integrals, amplitudes, source_order, target_order):
    x, y_lo, core, y_hi, z = place()
    wanted = flipped(flipped(rolled(target_order.reshape(4, 2, 2, 64), x), y_lo, 1), core, 2)
    wanted_x = wanted[..., :X_ROWS].transpose(2, 0, 1, 3).reshape(-1)
    wanted_y = wanted[..., X_ROWS:].transpose(2, 1, 0, 3).reshape(-1)
    held = flipped(rolled(source_order.reshape(2, 4, 128).transpose(1, 0, 2), z), y_hi, 1)
    order_in = ((0, 0), (3, 0), (1, 0), (0, 1), (2, 0), (3, 1), (1, 1), (2, 1))
    held = jnp.concatenate([held[at] for at in order_in])
    choose_x, choose_y = ((w[:, None] == held[None, :]).astype(jnp.bfloat16) for w in (wanted_x, wanted_y))

    v, chosen = lax.optimization_barrier((integrals, (choose_x, choose_y)))
    (keep_x, send_x), (keep_y, send_y) = (jnp.split(c, 2) for c in chosen)
    v, products = [v], []
    for columns in gather(amplitudes):
        parts, v = contract(v, columns)
        products += parts

    (term_y,) = order(send_y, products)
    got_y = shift(term_y, flip_core=True)
    (term_x,) = order(send_x, products)
    got_x = shift(term_x, flip_core=True)
    y_own, y_one = order(keep_y, products, [got_y], 2)
    y_sum = y_own + shift(y_one, flip_y=True)
    x_sum = sum_x(order(keep_x, products, [got_x], 4))

    part = y_sum.shape[0] // 4
    out_y = sum_x([y_sum[part * d : part * (d + 1)] for d in range(4)])
    part = x_sum.shape[0] // 2
    out_x = x_sum[:part] + shift(x_sum[part:], flip_y=True)
    return jnp.concatenate([out_x, out_y])


def solution(mesh):
    in_specs = (P("row", "col"), P("col", "row"), P(), P())
    return jax.shard_map(local, mesh=mesh, in_specs=in_specs, out_specs=P("col", "row"), check_vma=False)
```

```python
import functools

import jax
import jax.numpy as jnp
from jax import lax
from jax.experimental import pallas as pl
from jax.experimental.pallas import tpu as pltpu
from jax.sharding import PartitionSpec as P

AXES = ("row", "col")
MIB = 1 << 20
WHOLE = pl.BlockSpec(memory_space=pltpu.VMEM)
SCALARS = pl.BlockSpec(memory_space=pltpu.SMEM)
PAIRS, LANES, HALF = 1024, 128, 1024


def device_index(x, y, z, core):
    return ((y // 2) * 4 + z) * 16 + (x * 2 + y % 2) * 2 + core


def shift(array, dx=0, dy=0, dz=0, flip_y=False, flip_core=False):
    pairs = []
    for x in range(4):
        for y in range(4):
            for z in range(4):
                for core in range(2):
                    to_y = y ^ 1 if flip_y else (y + dy) % 4
                    to = device_index((x + dx) % 4, to_y, (z + dz) % 4, core ^ int(flip_core))
                    pairs.append((device_index(x, y, z, core), to))
    return lax.ppermute(array, AXES, pairs)


def place():
    row, col = lax.axis_index("row"), lax.axis_index("col")
    return col // 4, (col // 2) % 2, col % 2, row // 4, row % 4


def rolled(array, start):
    sizes = array.shape
    return lax.dynamic_slice(jnp.concatenate([array, array]), (start,) + (0,) * (array.ndim - 1), sizes)


def flipped(array, bit, axis):
    return jnp.where(bit == 0, array, jnp.flip(array, axis))


def parts_of(array):
    high = array.astype(jnp.bfloat16)
    return high, (array - high.astype(jnp.float32)).astype(jnp.bfloat16)


def stack_columns(layout, blocks, both):
    width = both.shape[1] // 2
    for at, start, size, row, col in layout:
        high, low = parts_of(blocks[at][start : start + size, :])
        both[row : row + size, col : col + 128] = high
        both[row : row + size, width + col : width + col + 128] = low


def product(vh, vl, both):
    width = both.shape[1] // 2
    dot = functools.partial(jnp.dot, preferred_element_type=jnp.float32)
    if width == 128:
        pair = dot(vh, both[...])
        return pair[:, :width] + pair[:, width:] + dot(vl, both[:, :width])
    return dot(vh, both[:, :width]) + dot(vh, both[:, width:]) + dot(vl, both[:, :width])


def store_rows(products, first, block):
    block = block.T
    for c in range(HALF // LANES):
        products[first : first + block.shape[0], c, :] = block[:, LANES * c : LANES * (c + 1)]


def first_kernel(layout, v_hbm, a_ref, vh_ref, vl_ref, *refs):
    halves, (both, total) = refs[:-2], refs[-2:]
    stack_columns(layout, [a_ref], both)
    ab, cd = vh_ref.shape
    tile = 256

    def body(v_ref):
        rows = pl.ds(pl.multiple_of(pl.program_id(0) * tile, tile), tile)
        vh, vl = parts_of(v_ref[...])
        vh_ref[rows, :], vl_ref[rows, :] = vh, vl
        total[rows, :] = product(vh, vl, both)

    block = pl.BlockSpec((tile, cd), lambda i: (i, 0), pipeline_mode=pl.Buffered(4))
    pltpu.emit_pipeline(body, grid=(ab // tile,), in_specs=[block], out_specs=[])(v_hbm)
    for i, products in enumerate(halves):
        store_rows(products, 0, total[HALF * i : HALF * (i + 1), :])


def contract_kernel(layout, n, which, first, vh_ref, vl_ref, *refs):
    blocks, halves, both = refs[:n], refs[-1 - len(which) : -1], refs[-1]
    stack_columns(layout, blocks, both)
    for i, products in zip(which, halves, strict=True):
        rows = pl.ds(HALF * i, HALF)
        store_rows(products, first, product(vh_ref[rows, :], vl_ref[rows, :], both))


def in_vmem(arrays):
    return [pltpu.with_memory_space_constraint(a, pltpu.VMEM) for a in arrays]


def contract(v, columns, which=(0, 1), into=()):
    layout, arrays = [], []
    for i, stack in enumerate(columns):
        row = 0
        for block in stack:
            layout.append((len(arrays), 0, block.shape[0], row, 128 * i))
            arrays.append(block)
            row += block.shape[0]
    ab, cd = v[0].shape
    width = 128 * len(columns)
    n_out = into[0].shape[0] if into else width
    scratch = [pltpu.VMEM((cd, 2 * width), jnp.bfloat16)]
    fresh = len(v) == 1
    if fresh:
        kernel = functools.partial(first_kernel, layout)
        inputs = [pltpu.with_memory_space_constraint(v[0], pltpu.HBM)]
        scratch += [pltpu.VMEM((ab, width), jnp.float32)]
    else:
        kernel = functools.partial(contract_kernel, layout, len(arrays), which, n_out - width)
        inputs = in_vmem(v)
    aliases = {} if fresh else {0: 0, 1: 1}
    aliases |= {2 + len(arrays) + i: 2 + i for i in range(len(into))}
    vh, vl, *products = pl.pallas_call(
        kernel,
        in_specs=[pl.BlockSpec(memory_space=pl.ANY) if fresh else WHOLE] * len(inputs)
        + [WHOLE] * (len(arrays) + len(into)),
        out_specs=[WHOLE] * (2 + len(which)),
        out_shape=[pltpu.VMEM((ab, cd), jnp.bfloat16)] * 2
        + [pltpu.VMEM((n_out, HALF // LANES, LANES), jnp.float32)] * len(which),
        input_output_aliases=aliases,
        scratch_shapes=scratch,
        compiler_params=pltpu.CompilerParams(vmem_limit_bytes=(18 if fresh else 14) * MIB),
        cost_estimate=pl.CostEstimate(flops=6 * width * HALF * len(which) * cd, bytes_accessed=0, transcendentals=0),
        name="contract",
    )(*inputs, *in_vmem(arrays), *in_vmem(into))
    return [vh, vl], products


def merge_kernel(*refs):
    out, row = refs[-1], 0
    for ref in refs[:-1]:
        out[row : row + ref.shape[0]] = ref[...]
        row += ref.shape[0]


def merge(products):
    return pl.pallas_call(
        merge_kernel,
        in_specs=[WHOLE] * len(products),
        out_specs=WHOLE,
        out_shape=pltpu.VMEM((PAIRS, *products[0].shape[1:]), jnp.float32),
        compiler_params=pltpu.CompilerParams(vmem_limit_bytes=4 * MIB),
        cost_estimate=pl.CostEstimate(flops=0, bytes_accessed=0, transcendentals=0),
        name="merge",
    )(*in_vmem(products))


def pack_kernel(layout, *refs):
    for at, out, row, start, size in layout:
        refs[out][row : row + size, :] = refs[at][start : start + size, :]


def pack(*stacks):
    arrays = [block[0] for stack in stacks for block in stack]
    arrays = [a for i, a in enumerate(arrays) if not any(a is b for b in arrays[:i])]
    layout, shapes = [], []
    for out, stack in enumerate(stacks):
        row = 0
        for array, start, size in stack:
            at = next(i for i, a in enumerate(arrays) if a is array)
            layout.append((at, len(arrays) + out, row, start, size))
            row += size
        shapes.append(pltpu.VMEM((row, arrays[0].shape[1]), jnp.float32))
    return pl.pallas_call(
        functools.partial(pack_kernel, layout),
        in_specs=[WHOLE] * len(arrays),
        out_specs=[WHOLE] * len(stacks),
        out_shape=shapes,
        compiler_params=pltpu.CompilerParams(vmem_limit_bytes=5 * MIB),
        cost_estimate=pl.CostEstimate(flops=0, bytes_accessed=0, transcendentals=0),
        name="pack",
    )(*[pltpu.with_memory_space_constraint(a, pltpu.VMEM) for a in arrays])


def find_kernel(held_ref, wanted_ref, at_ref, inverse):
    @pl.loop(0, PAIRS, unroll=16)
    def _(p):
        inverse[held_ref[p]] = p

    @pl.loop(0, at_ref.shape[0], unroll=16)
    def _(q):
        at_ref[q] = inverse[wanted_ref[q]]


def find(held, wanted):
    return pl.pallas_call(
        find_kernel,
        in_specs=[SCALARS] * 2,
        out_specs=SCALARS,
        out_shape=jax.ShapeDtypeStruct(wanted.shape, jnp.int32),
        scratch_shapes=[pltpu.SMEM((PAIRS,), jnp.int32)],
        compiler_params=pltpu.CompilerParams(vmem_limit_bytes=MIB),
        cost_estimate=pl.CostEstimate(flops=0, bytes_accessed=0, transcendentals=0),
        name="find",
    )(held, wanted)


def order_kernel(first, n_got, at_ref, products, *refs):
    got, outs = refs[:n_got], refs[n_got:]
    row = 0
    for ref in outs:

        @pl.loop(0, ref.shape[0], unroll=8)
        def _(q, ref=ref, row=row):
            block = products[at_ref[first + row + q]]
            for term in got:
                block = block + term[row + q]
            ref[q] = block

        row += ref.shape[0]


def order(at, products, first, sizes, got=()):
    inputs = in_vmem((products, *got))
    return pl.pallas_call(
        functools.partial(order_kernel, first, len(got)),
        in_specs=[SCALARS] + [WHOLE] * len(inputs),
        out_specs=[WHOLE] * len(sizes),
        out_shape=[pltpu.VMEM((n, *products.shape[1:]), jnp.float32) for n in sizes],
        compiler_params=pltpu.CompilerParams(vmem_limit_bytes=4 * MIB),
        cost_estimate=pl.CostEstimate(flops=0, bytes_accessed=0, transcendentals=0),
        name="order",
    )(at, *inputs)


def after(value, *others):
    return lax.optimization_barrier((value, others))[0]


def products_of(v, a, held, wanted):
    mid = a.shape[0] // 2
    zm, zp, y0 = shift(a, dz=1), shift(a, dz=-1), shift(a, dy=2)
    at = find(held, wanted)
    v, own = contract([after(v, at)], ([a],))

    zm_low, zm_high, zp_high, y0_low = pack(
        *(((block, row, mid),) for block, row in ((after(zm, own), 0), (zm, mid), (zp, mid), (y0, 0)))
    )
    y_zm_high, z2_low, z2_high = shift(zm_high, dy=2), shift(zm_low, dz=1), shift(zp_high, dz=-1)
    v, near = contract(v, ([zm], [zp]))

    y_zm_low, y_zp_low = shift(after(y0_low, near), dz=1), shift(after(y0_low, near), dz=-1)
    y_zp_high = shift(after(zp_high, near, y_zm_high), dy=2)
    v, far = contract(v, ([y0], [z2_low, z2_high]))

    y_z2_low, y_z2_high = shift(after(y_zm_low, far), dz=1), shift(after(y_zp_high, far), dz=-1)
    v, beyond = contract(v, ([y_zm_low, y_zm_high], [y_zp_low, y_zp_high]))
    low, high = (merge(list(parts)) for parts in zip(own, near, far, beyond, strict=True))
    v, (low,) = contract(v, ([y_z2_low, y_z2_high],), (0,), [low])
    return low, lambda *others: contract(after(v, *others), ([y_z2_low, y_z2_high],), (1,), [high])[1][0], at


def add_rows(block, more, row):
    return lax.dynamic_update_slice_in_dim(block, block[row : row + more.shape[0]] + more, row, 0)


def ring_x(own, up, far_up, far_down, down):
    n = far_up.shape[0]
    far_up, far_down = shift(far_up, dx=1), shift(far_down, dx=-1)
    return own, shift(add_rows(up, far_up, 0), dx=1), shift(add_rows(down, far_down, n), dx=-1)


def spread_x(blocks):
    return [blocks[0], shift(blocks[2], dx=2), shift(blocks[1], dx=1), shift(blocks[3], dx=-1)]


def local(integrals, amplitudes, source_order, target_order):
    x, y_lo, core, y_hi, z = place()
    wanted = flipped(flipped(rolled(target_order.reshape(4, 2, 2, 64), x), y_lo, 1), core, 2)
    wanted_x = wanted.transpose(2, 0, 1, 3).reshape(-1)
    wanted_y = wanted.transpose(2, 1, 0, 3).reshape(-1)
    held = flipped(rolled(source_order.reshape(2, 4, 128).transpose(1, 0, 2), z), y_hi, 1)
    order_in = ((0, 0), (3, 0), (1, 0), (0, 1), (2, 0), (3, 1), (1, 1), (2, 1))
    held = jnp.concatenate([held[at] for at in order_in])
    products, more, at = products_of(integrals, amplitudes, held, jnp.concatenate([wanted_x, wanted_y]))

    n = PAIRS // 2
    (term_y,) = order(at, products, PAIRS + n, [n])
    got_y = shift(term_y, flip_core=True)
    y_own, y_one = order(at, products, PAIRS, [n // 2] * 2, [got_y])
    y_sum = y_own + shift(y_one, flip_y=True)

    products = more(term_y)
    (term_x,) = order(at, products, n, [n])
    got_x = shift(term_x, flip_core=True)
    x_terms = ring_x(*order(at, after(products, y_one), 0, [n // 4] * 2 + [n // 8] * 2 + [n // 4], [got_x]))

    part = n // 8
    y_terms = spread_x([y_sum[part * d : part * (d + 1)] for d in range(4)])
    out_y, x_sum = sum(y_terms), sum(after(x_terms, y_terms[1]))
    out_x = x_sum[:part] + shift(x_sum[part:], flip_y=True)
    return jnp.concatenate([out_y.reshape(part, -1), out_x.reshape(part, -1)], axis=1)


def solution(mesh):
    in_specs = (P("row", "col"), P("col", "row"), P(), P())
    return jax.shard_map(local, mesh=mesh, in_specs=in_specs, out_specs=P("col", "row"), check_vma=False)
```

```python
import functools

import jax
import jax.numpy as jnp
from jax import lax
from jax.experimental import pallas as pl
from jax.experimental.pallas import tpu as pltpu
from jax.sharding import PartitionSpec as P

AXES = ("row", "col")
MIB = 1 << 20
WHOLE = pl.BlockSpec(memory_space=pltpu.VMEM)
SCALARS = pl.BlockSpec(memory_space=pltpu.SMEM)
PAIRS, LANES, HALF = 1024, 128, 1024


def device_index(x, y, z, core):
    return ((y // 2) * 4 + z) * 16 + (x * 2 + y % 2) * 2 + core


def shift(array, dx=0, dy=0, dz=0, flip_y=False, flip_core=False):
    pairs = []
    for x in range(4):
        for y in range(4):
            for z in range(4):
                for core in range(2):
                    to_y = y ^ 1 if flip_y else (y + dy) % 4
                    to = device_index((x + dx) % 4, to_y, (z + dz) % 4, core ^ int(flip_core))
                    pairs.append((device_index(x, y, z, core), to))
    return lax.ppermute(array, AXES, pairs)


def place():
    row, col = lax.axis_index("row"), lax.axis_index("col")
    return col // 4, (col // 2) % 2, col % 2, row // 4, row % 4


def rolled(array, start):
    sizes = array.shape
    return lax.dynamic_slice(jnp.concatenate([array, array]), (start,) + (0,) * (array.ndim - 1), sizes)


def flipped(array, bit, axis):
    return jnp.where(bit == 0, array, jnp.flip(array, axis))


def parts_of(array):
    high = array.astype(jnp.bfloat16)
    return high, (array - high.astype(jnp.float32)).astype(jnp.bfloat16)


def stack_columns(layout, blocks, both):
    width = both.shape[1] // 2
    for at, start, size, row, col in layout:
        high, low = parts_of(blocks[at][start : start + size, :])
        both[row : row + size, col : col + 128] = high
        both[row : row + size, width + col : width + col + 128] = low


def product(vh, vl, both):
    width = both.shape[1] // 2
    dot = functools.partial(jnp.dot, preferred_element_type=jnp.float32)
    if width == 128:
        pair = dot(vh, both[...])
        return pair[:, :width] + pair[:, width:] + dot(vl, both[:, :width])
    return dot(vh, both[:, :width]) + dot(vh, both[:, width:]) + dot(vl, both[:, :width])


def store_rows(products, first, block):
    block = block.T
    for c in range(HALF // LANES):
        products[first : first + block.shape[0], c, :] = block[:, LANES * c : LANES * (c + 1)]


def first_kernel(layout, v_hbm, a_ref, vh_ref, vl_ref, *refs):
    halves, (both, total) = refs[:-2], refs[-2:]
    stack_columns(layout, [a_ref], both)
    ab, cd = vh_ref.shape
    tile = 256

    def body(v_ref):
        rows = pl.ds(pl.multiple_of(pl.program_id(0) * tile, tile), tile)
        vh, vl = parts_of(v_ref[...])
        vh_ref[rows, :], vl_ref[rows, :] = vh, vl
        total[rows, :] = product(vh, vl, both)

    block = pl.BlockSpec((tile, cd), lambda i: (i, 0), pipeline_mode=pl.Buffered(4))
    pltpu.emit_pipeline(body, grid=(ab // tile,), in_specs=[block], out_specs=[])(v_hbm)
    for i, products in enumerate(halves):
        store_rows(products, 0, total[HALF * i : HALF * (i + 1), :])


def contract_kernel(layout, n, which, first, vh_ref, vl_ref, *refs):
    blocks, halves, both = refs[:n], refs[-1 - len(which) : -1], refs[-1]
    stack_columns(layout, blocks, both)
    for i, products in zip(which, halves, strict=True):
        rows = pl.ds(HALF * i, HALF)
        store_rows(products, first, product(vh_ref[rows, :], vl_ref[rows, :], both))


def in_vmem(arrays):
    return [pltpu.with_memory_space_constraint(a, pltpu.VMEM) for a in arrays]


def contract(v, columns, which=(0, 1), into=()):
    layout, arrays = [], []
    for i, stack in enumerate(columns):
        row = 0
        for block in stack:
            layout.append((len(arrays), 0, block.shape[0], row, 128 * i))
            arrays.append(block)
            row += block.shape[0]
    ab, cd = v[0].shape
    width = 128 * len(columns)
    n_out = into[0].shape[0] if into else width
    scratch = [pltpu.VMEM((cd, 2 * width), jnp.bfloat16)]
    fresh = len(v) == 1
    if fresh:
        kernel = functools.partial(first_kernel, layout)
        inputs = [pltpu.with_memory_space_constraint(v[0], pltpu.HBM)]
        scratch += [pltpu.VMEM((ab, width), jnp.float32)]
    else:
        kernel = functools.partial(contract_kernel, layout, len(arrays), which, n_out - width)
        inputs = in_vmem(v)
    aliases = {} if fresh else {0: 0, 1: 1}
    aliases |= {2 + len(arrays) + i: 2 + i for i in range(len(into))}
    vh, vl, *products = pl.pallas_call(
        kernel,
        in_specs=[pl.BlockSpec(memory_space=pl.ANY) if fresh else WHOLE] * len(inputs)
        + [WHOLE] * (len(arrays) + len(into)),
        out_specs=[WHOLE] * (2 + len(which)),
        out_shape=[pltpu.VMEM((ab, cd), jnp.bfloat16)] * 2
        + [pltpu.VMEM((n_out, HALF // LANES, LANES), jnp.float32)] * len(which),
        input_output_aliases=aliases,
        scratch_shapes=scratch,
        compiler_params=pltpu.CompilerParams(vmem_limit_bytes=(18 if fresh else 14) * MIB),
        cost_estimate=pl.CostEstimate(flops=6 * width * HALF * len(which) * cd, bytes_accessed=0, transcendentals=0),
        name="contract",
    )(*inputs, *in_vmem(arrays), *in_vmem(into))
    return [vh, vl], products


def merge_kernel(*refs):
    out, row = refs[-1], 0
    for ref in refs[:-1]:
        out[row : row + ref.shape[0]] = ref[...]
        row += ref.shape[0]


def merge(products):
    return pl.pallas_call(
        merge_kernel,
        in_specs=[WHOLE] * len(products),
        out_specs=WHOLE,
        out_shape=pltpu.VMEM((PAIRS, *products[0].shape[1:]), jnp.float32),
        compiler_params=pltpu.CompilerParams(vmem_limit_bytes=4 * MIB),
        cost_estimate=pl.CostEstimate(flops=0, bytes_accessed=0, transcendentals=0),
        name="merge",
    )(*in_vmem(products))


def pack_kernel(layout, *refs):
    for at, out, row, start, size in layout:
        refs[out][row : row + size, :] = refs[at][start : start + size, :]


def pack(*stacks):
    arrays = [block[0] for stack in stacks for block in stack]
    arrays = [a for i, a in enumerate(arrays) if not any(a is b for b in arrays[:i])]
    layout, shapes = [], []
    for out, stack in enumerate(stacks):
        row = 0
        for array, start, size in stack:
            at = next(i for i, a in enumerate(arrays) if a is array)
            layout.append((at, len(arrays) + out, row, start, size))
            row += size
        shapes.append(pltpu.VMEM((row, arrays[0].shape[1]), jnp.float32))
    return pl.pallas_call(
        functools.partial(pack_kernel, layout),
        in_specs=[WHOLE] * len(arrays),
        out_specs=[WHOLE] * len(stacks),
        out_shape=shapes,
        compiler_params=pltpu.CompilerParams(vmem_limit_bytes=5 * MIB),
        cost_estimate=pl.CostEstimate(flops=0, bytes_accessed=0, transcendentals=0),
        name="pack",
    )(*[pltpu.with_memory_space_constraint(a, pltpu.VMEM) for a in arrays])


def find_kernel(held_ref, wanted_ref, at_ref, inverse):
    @pl.loop(0, PAIRS, unroll=16)
    def _(p):
        inverse[held_ref[p]] = p

    @pl.loop(0, at_ref.shape[0], unroll=16)
    def _(q):
        at_ref[q] = inverse[wanted_ref[q]]


def find(held, wanted):
    return pl.pallas_call(
        find_kernel,
        in_specs=[SCALARS] * 2,
        out_specs=SCALARS,
        out_shape=jax.ShapeDtypeStruct(wanted.shape, jnp.int32),
        scratch_shapes=[pltpu.SMEM((PAIRS,), jnp.int32)],
        compiler_params=pltpu.CompilerParams(vmem_limit_bytes=MIB),
        cost_estimate=pl.CostEstimate(flops=0, bytes_accessed=0, transcendentals=0),
        name="find",
    )(held, wanted)


def order_kernel(first, n_got, at_ref, products, *refs):
    got, outs = refs[:n_got], refs[n_got:]
    row = 0
    for ref in outs:

        @pl.loop(0, ref.shape[0], unroll=32)
        def _(q, ref=ref, row=row):
            block = products[at_ref[first + row + q]]
            for term in got:
                block = block + term[row + q]
            ref[q] = block

        row += ref.shape[0]


def order(at, products, first, sizes, got=()):
    inputs = in_vmem((products, *got))
    return pl.pallas_call(
        functools.partial(order_kernel, first, len(got)),
        in_specs=[SCALARS] + [WHOLE] * len(inputs),
        out_specs=[WHOLE] * len(sizes),
        out_shape=[pltpu.VMEM((n, *products.shape[1:]), jnp.float32) for n in sizes],
        compiler_params=pltpu.CompilerParams(vmem_limit_bytes=4 * MIB),
        cost_estimate=pl.CostEstimate(flops=0, bytes_accessed=0, transcendentals=0),
        name="order",
    )(at, *inputs)


def after(value, *others):
    return lax.optimization_barrier((value, others))[0]


def products_of(v, a, held, wanted):
    mid = a.shape[0] // 2
    zm, zp, y0 = shift(a, dz=1), shift(a, dz=-1), shift(a, dy=2)
    at = find(held, wanted)
    v, own = contract([after(v, at)], ([a],))

    zm_low, zm_high, zp_high, y0_low = pack(
        *(((block, row, mid),) for block, row in ((after(zm, own), 0), (zm, mid), (zp, mid), (y0, 0)))
    )
    y_zm_high, z2_low, z2_high = shift(zm_high, dy=2), shift(zm_low, dz=1), shift(zp_high, dz=-1)
    v, near = contract(v, ([zm], [zp]))

    y_zm_low, y_zp_low = shift(after(y0_low, near), dz=1), shift(after(y0_low, near), dz=-1)
    y_zp_high = shift(after(zp_high, near, y_zm_high), dy=2)
    v, far = contract(v, ([y0], [z2_low, z2_high]))

    y_z2_low, y_z2_high = shift(after(y_zm_low, far), dz=1), shift(after(y_zp_high, far), dz=-1)
    v, beyond = contract(v, ([y_zm_low, y_zm_high], [y_zp_low, y_zp_high]))
    low, high = (merge(list(parts)) for parts in zip(own, near, far, beyond, strict=True))
    v, (low,) = contract(v, ([y_z2_low, y_z2_high],), (0,), [low])
    return low, lambda *others: contract(after(v, *others), ([y_z2_low, y_z2_high],), (1,), [high])[1][0], at


def add_rows(block, more, row):
    return lax.dynamic_update_slice_in_dim(block, block[row : row + more.shape[0]] + more, row, 0)


def ring_x(own, up, far_up, far_down, down):
    n = far_up.shape[0]
    far_up, far_down = lax.optimization_barrier((shift(far_up, dx=1), shift(far_down, dx=-1)))
    return own, shift(add_rows(up, far_up, 0), dx=1), shift(add_rows(down, far_down, n), dx=-1)


def spread_x(blocks):
    return [blocks[0], shift(blocks[2], dx=2), shift(blocks[1], dx=1), shift(blocks[3], dx=-1)]


def local(integrals, amplitudes, source_order, target_order):
    x, y_lo, core, y_hi, z = place()
    wanted = flipped(flipped(rolled(target_order.reshape(4, 2, 2, 64), x), y_lo, 1), core, 2)
    wanted_x = wanted.transpose(2, 0, 1, 3).reshape(-1)
    wanted_y = wanted.transpose(2, 1, 0, 3).reshape(-1)
    held = flipped(rolled(source_order.reshape(2, 4, 128).transpose(1, 0, 2), z), y_hi, 1)
    order_in = ((0, 0), (3, 0), (1, 0), (0, 1), (2, 0), (3, 1), (1, 1), (2, 1))
    held = jnp.concatenate([held[at] for at in order_in])
    products, more, at = products_of(integrals, amplitudes, held, jnp.concatenate([wanted_x, wanted_y]))

    n = PAIRS // 2
    (term_y,) = order(at, products, PAIRS + n, [n])
    got_y = shift(term_y, flip_core=True)
    y_own, y_one = order(at, products, PAIRS, [n // 2] * 2, [got_y])
    y_sum = y_own + shift(y_one, flip_y=True)

    products = more(term_y)
    (term_x,) = order(at, products, n, [n])
    got_x = shift(term_x, flip_core=True)
    x_terms = ring_x(*order(at, after(products, y_one), 0, [n // 4] * 2 + [n // 8] * 2 + [n // 4], [got_x]))

    part = n // 8
    half = part // 2
    y_rows = (0, part), (part, 2 * part), (2 * part, 2 * part + half), (2 * part + half, 3 * part), (3 * part, 4 * part)
    y_terms = ring_x(*[y_sum[i:j] for i, j in y_rows])
    out_y, x_sum = sum(y_terms), sum(after(x_terms, y_sum))
    out_x = x_sum[:part] + shift(x_sum[part:], flip_y=True)
    return jnp.concatenate([out_y.reshape(part, -1), out_x.reshape(part, -1)], axis=1)


def solution(mesh):
    in_specs = (P("row", "col"), P("col", "row"), P(), P())
    return jax.shard_map(local, mesh=mesh, in_specs=in_specs, out_specs=P("col", "row"), check_vma=False)
```

```python
import functools

import jax
import jax.numpy as jnp
from jax import lax
from jax.experimental import pallas as pl
from jax.experimental.pallas import tpu as pltpu
from jax.sharding import PartitionSpec as P

AXES = ("row", "col")
MIB = 1 << 20
WHOLE = pl.BlockSpec(memory_space=pltpu.VMEM)
SCALARS = pl.BlockSpec(memory_space=pltpu.SMEM)
PAIRS, LANES, HALF = 1024, 128, 1024


def device_index(x, y, z, core):
    return ((y // 2) * 4 + z) * 16 + (x * 2 + y % 2) * 2 + core


def shift(array, dx=0, dy=0, dz=0, flip_y=False, flip_core=False):
    pairs = []
    for x in range(4):
        for y in range(4):
            for z in range(4):
                for core in range(2):
                    to_y = y ^ 1 if flip_y else (y + dy) % 4
                    to = device_index((x + dx) % 4, to_y, (z + dz) % 4, core ^ int(flip_core))
                    pairs.append((device_index(x, y, z, core), to))
    return lax.ppermute(array, AXES, pairs)


def place():
    row, col = lax.axis_index("row"), lax.axis_index("col")
    return col // 4, (col // 2) % 2, col % 2, row // 4, row % 4


def rolled(array, start):
    sizes = array.shape
    return lax.dynamic_slice(jnp.concatenate([array, array]), (start,) + (0,) * (array.ndim - 1), sizes)


def flipped(array, bit, axis):
    return jnp.where(bit == 0, array, jnp.flip(array, axis))


def parts_of(array):
    high = array.astype(jnp.bfloat16)
    return high, (array - high.astype(jnp.float32)).astype(jnp.bfloat16)


def stack_columns(layout, blocks, both):
    width = both.shape[1] // 2
    for at, start, size, row, col in layout:
        high, low = parts_of(blocks[at][start : start + size, :])
        both[row : row + size, col : col + 128] = high
        both[row : row + size, width + col : width + col + 128] = low


def product(vh, vl, both):
    width = both.shape[1] // 2
    dot = functools.partial(jnp.dot, preferred_element_type=jnp.float32)
    if width == 128:
        pair = dot(vh, both[...])
        return pair[:, :width] + pair[:, width:] + dot(vl, both[:, :width])
    return dot(vh, both[:, :width]) + dot(vh, both[:, width:]) + dot(vl, both[:, :width])


def store_rows(products, first, block):
    block = block.T
    for c in range(HALF // LANES):
        products[first : first + block.shape[0], c, :] = block[:, LANES * c : LANES * (c + 1)]


def first_kernel(layout, v_hbm, a_ref, vh_ref, vl_ref, *refs):
    halves, (both, total) = refs[:-2], refs[-2:]
    stack_columns(layout, [a_ref], both)
    ab, cd = vh_ref.shape
    tile = 256

    def body(v_ref):
        rows = pl.ds(pl.multiple_of(pl.program_id(0) * tile, tile), tile)
        vh, vl = parts_of(v_ref[...])
        vh_ref[rows, :], vl_ref[rows, :] = vh, vl
        total[rows, :] = product(vh, vl, both)

    block = pl.BlockSpec((tile, cd), lambda i: (i, 0), pipeline_mode=pl.Buffered(4))
    pltpu.emit_pipeline(body, grid=(ab // tile,), in_specs=[block], out_specs=[])(v_hbm)
    for i, products in enumerate(halves):
        store_rows(products, 0, total[HALF * i : HALF * (i + 1), :])


def contract_kernel(layout, n, which, first, vh_ref, vl_ref, *refs):
    blocks, halves, both = refs[:n], refs[-1 - len(which) : -1], refs[-1]
    stack_columns(layout, blocks, both)
    for i, products in zip(which, halves, strict=True):
        rows = pl.ds(HALF * i, HALF)
        store_rows(products, first, product(vh_ref[rows, :], vl_ref[rows, :], both))


def in_vmem(arrays):
    return [pltpu.with_memory_space_constraint(a, pltpu.VMEM) for a in arrays]


def contract(v, columns, which=(0, 1), into=()):
    layout, arrays = [], []
    for i, stack in enumerate(columns):
        row = 0
        for block in stack:
            layout.append((len(arrays), 0, block.shape[0], row, 128 * i))
            arrays.append(block)
            row += block.shape[0]
    ab, cd = v[0].shape
    width = 128 * len(columns)
    n_out = into[0].shape[0] if into else width
    scratch = [pltpu.VMEM((cd, 2 * width), jnp.bfloat16)]
    fresh = len(v) == 1
    if fresh:
        kernel = functools.partial(first_kernel, layout)
        inputs = [pltpu.with_memory_space_constraint(v[0], pltpu.HBM)]
        scratch += [pltpu.VMEM((ab, width), jnp.float32)]
    else:
        kernel = functools.partial(contract_kernel, layout, len(arrays), which, n_out - width)
        inputs = in_vmem(v)
    aliases = {} if fresh else {0: 0, 1: 1}
    aliases |= {2 + len(arrays) + i: 2 + i for i in range(len(into))}
    vh, vl, *products = pl.pallas_call(
        kernel,
        in_specs=[pl.BlockSpec(memory_space=pl.ANY) if fresh else WHOLE] * len(inputs)
        + [WHOLE] * (len(arrays) + len(into)),
        out_specs=[WHOLE] * (2 + len(which)),
        out_shape=[pltpu.VMEM((ab, cd), jnp.bfloat16)] * 2
        + [pltpu.VMEM((n_out, HALF // LANES, LANES), jnp.float32)] * len(which),
        input_output_aliases=aliases,
        scratch_shapes=scratch,
        compiler_params=pltpu.CompilerParams(vmem_limit_bytes=(18 if fresh else 14) * MIB),
        cost_estimate=pl.CostEstimate(flops=6 * width * HALF * len(which) * cd, bytes_accessed=0, transcendentals=0),
        name="contract",
    )(*inputs, *in_vmem(arrays), *in_vmem(into))
    return [vh, vl], products


def merge_kernel(*refs):
    out, row = refs[-1], 0
    for ref in refs[:-1]:
        out[row : row + ref.shape[0]] = ref[...]
        row += ref.shape[0]


def merge(products):
    return pl.pallas_call(
        merge_kernel,
        in_specs=[WHOLE] * len(products),
        out_specs=WHOLE,
        out_shape=pltpu.VMEM((PAIRS, *products[0].shape[1:]), jnp.float32),
        compiler_params=pltpu.CompilerParams(vmem_limit_bytes=4 * MIB),
        cost_estimate=pl.CostEstimate(flops=0, bytes_accessed=0, transcendentals=0),
        name="merge",
    )(*in_vmem(products))


def pack_kernel(layout, *refs):
    for at, out, row, start, size in layout:
        refs[out][row : row + size, :] = refs[at][start : start + size, :]


def pack(*stacks):
    arrays = [block[0] for stack in stacks for block in stack]
    arrays = [a for i, a in enumerate(arrays) if not any(a is b for b in arrays[:i])]
    layout, shapes = [], []
    for out, stack in enumerate(stacks):
        row = 0
        for array, start, size in stack:
            at = next(i for i, a in enumerate(arrays) if a is array)
            layout.append((at, len(arrays) + out, row, start, size))
            row += size
        shapes.append(pltpu.VMEM((row, arrays[0].shape[1]), jnp.float32))
    return pl.pallas_call(
        functools.partial(pack_kernel, layout),
        in_specs=[WHOLE] * len(arrays),
        out_specs=[WHOLE] * len(stacks),
        out_shape=shapes,
        compiler_params=pltpu.CompilerParams(vmem_limit_bytes=5 * MIB),
        cost_estimate=pl.CostEstimate(flops=0, bytes_accessed=0, transcendentals=0),
        name="pack",
    )(*[pltpu.with_memory_space_constraint(a, pltpu.VMEM) for a in arrays])


def find_kernel(held_ref, wanted_ref, at_ref, inverse):
    @pl.loop(0, PAIRS, unroll=16)
    def _(p):
        inverse[held_ref[p]] = p

    @pl.loop(0, at_ref.shape[0], unroll=16)
    def _(q):
        at_ref[q] = inverse[wanted_ref[q]]


def find(held, wanted):
    return pl.pallas_call(
        find_kernel,
        in_specs=[SCALARS] * 2,
        out_specs=SCALARS,
        out_shape=jax.ShapeDtypeStruct(wanted.shape, jnp.int32),
        scratch_shapes=[pltpu.SMEM((PAIRS,), jnp.int32)],
        compiler_params=pltpu.CompilerParams(vmem_limit_bytes=MIB),
        cost_estimate=pl.CostEstimate(flops=0, bytes_accessed=0, transcendentals=0),
        name="find",
    )(held, wanted)


def order_kernel(first, n_got, at_ref, products, *refs):
    got, outs = refs[:n_got], refs[n_got:]
    row = 0
    for ref in outs:

        @pl.loop(0, ref.shape[0], unroll=32)
        def _(q, ref=ref, row=row):
            block = products[at_ref[first + row + q]]
            for term in got:
                block = block + term[row + q]
            ref[q] = block

        row += ref.shape[0]


def order(at, products, first, sizes, got=()):
    inputs = in_vmem((products, *got))
    return pl.pallas_call(
        functools.partial(order_kernel, first, len(got)),
        in_specs=[SCALARS] + [WHOLE] * len(inputs),
        out_specs=[WHOLE] * len(sizes),
        out_shape=[pltpu.VMEM((n, *products.shape[1:]), jnp.float32) for n in sizes],
        compiler_params=pltpu.CompilerParams(vmem_limit_bytes=4 * MIB),
        cost_estimate=pl.CostEstimate(flops=0, bytes_accessed=0, transcendentals=0),
        name="order",
    )(at, *inputs)


def after(value, *others):
    return lax.optimization_barrier((value, others))[0]


def products_of(v, a, held, wanted):
    mid = a.shape[0] // 2
    zm, zp, y0 = shift(a, dz=1), shift(a, dz=-1), shift(a, dy=2)
    at = find(held, wanted)
    v, own = contract([after(v, at)], ([a],))

    zm_low, zm_high, zp_high = pack(*(((block, row, mid),) for block, row in ((after(zm, own), 0), (zm, mid), (zp, mid))))
    y_zm_high, z2_low, z2_high = shift(zm_high, dy=2), shift(zm_low, dz=1), shift(zp_high, dz=-1)
    v, near = contract(v, ([zm], [zp]))

    (y0_low,) = pack(((after(y0, near), 0, mid),))
    y_zm_low, y_zp_low = shift(after(y0_low, near), dz=1), shift(after(y0_low, near), dz=-1)
    y_zp_high = shift(after(zp_high, near, y_zm_high), dy=2)
    v, far = contract(v, ([y0], [z2_low, z2_high]))

    y_z2_low, y_z2_high = shift(after(y_zm_low, far), dz=1), shift(after(y_zp_high, far), dz=-1)
    v, beyond = contract(v, ([y_zm_low, y_zm_high], [y_zp_low, y_zp_high]))
    low, high = (merge(list(parts)) for parts in zip(own, near, far, beyond, strict=True))
    v, (low,) = contract(v, ([y_z2_low, y_z2_high],), (0,), [low])
    return low, lambda *others: contract(after(v, *others), ([y_z2_low, y_z2_high],), (1,), [high])[1][0], at


def add_rows(block, more, row):
    return lax.dynamic_update_slice_in_dim(block, block[row : row + more.shape[0]] + more, row, 0)


def ring_x(own, up, far_up, far_down, down):
    n = far_up.shape[0]
    far_up, far_down = lax.optimization_barrier((shift(far_up, dx=1), shift(far_down, dx=-1)))
    return own, shift(add_rows(up, far_up, 0), dx=1), shift(add_rows(down, far_down, n), dx=-1)


def spread_x(blocks):
    return [blocks[0], shift(blocks[2], dx=2), shift(blocks[1], dx=1), shift(blocks[3], dx=-1)]


def local(integrals, amplitudes, source_order, target_order):
    x, y_lo, core, y_hi, z = place()
    wanted = flipped(flipped(rolled(target_order.reshape(4, 2, 2, 64), x), y_lo, 1), core, 2)
    wanted_x = wanted.transpose(2, 0, 1, 3).reshape(-1)
    wanted_y = wanted.transpose(2, 1, 0, 3).reshape(-1)
    held = flipped(rolled(source_order.reshape(2, 4, 128).transpose(1, 0, 2), z), y_hi, 1)
    order_in = ((0, 0), (3, 0), (1, 0), (0, 1), (2, 0), (3, 1), (1, 1), (2, 1))
    held = jnp.concatenate([held[at] for at in order_in])
    products, more, at = products_of(integrals, amplitudes, held, jnp.concatenate([wanted_x, wanted_y]))

    n = PAIRS // 2
    (term_y,) = order(at, products, PAIRS + n, [n])
    got_y = shift(term_y, flip_core=True)
    y_own, y_one = order(at, products, PAIRS, [n // 2] * 2, [got_y])
    y_sum = y_own + shift(y_one, flip_y=True)

    products = more(term_y)
    (term_x,) = order(at, products, n, [n])
    got_x = shift(term_x, flip_core=True)
    x_terms = ring_x(*order(at, after(products, y_one), 0, [n // 4] * 2 + [n // 8] * 2 + [n // 4], [got_x]))

    part = n // 8
    half = part // 2
    y_rows = (0, part), (part, 2 * part), (2 * part, 2 * part + half), (2 * part + half, 3 * part), (3 * part, 4 * part)
    y_terms = ring_x(*[y_sum[i:j] for i, j in y_rows])
    out_y, x_sum = sum(y_terms), sum(after(x_terms, y_sum))
    out_x = x_sum[:part] + shift(x_sum[part:], flip_y=True)
    return jnp.concatenate([out_y.reshape(part, -1), out_x.reshape(part, -1)], axis=1)


def solution(mesh):
    in_specs = (P("row", "col"), P("col", "row"), P(), P())
    return jax.shard_map(local, mesh=mesh, in_specs=in_specs, out_specs=P("col", "row"), check_vma=False)
```
